32 devices in a mesh: group: 2 (over y), view: 4 (over z), tok: 4 (over x, core).
Axes of the slice: x: 2, y: 2, z: 4, core: 2. Of those that a mesh axis runs over, the one named last changes fastest.
Arguments:
- query_rows: bfloat16 [8192, 384], P(('group', 'view', 'tok')), parts along dimension 0, may hold values from -6 to 6
- key_rows: bfloat16 [8192, 384], P(('group', 'view', 'tok')), parts along dimension 0, may hold values from -6 to 6
- value_rows: bfloat16 [8192, 384], P(('group', 'view', 'tok')), parts along dimension 0, may hold values from -6 to 6
- token_rates: float32 [8192], P(('group', 'view', 'tok')), parts along dimension 0, may hold values from 0.25 to 4
- output_cot: bfloat16 [8192, 384], P(('group', 'view', 'tok')), parts along dimension 0, may hold values from -6 to 6
- w_gate: float32 [768, 384], replicated, may hold values from -0.3125 to 0.3125
- w_up: float32 [768, 384], replicated, may hold values from -0.3125 to 0.3125
- w_down: float32 [768, 384], replicated, may hold values from -0.21875 to 0.21875
Outputs:
- queries_grad: bfloat16 [8192, 384], P(('group', 'view', 'tok')), parts along dimension 0
- keys_grad: bfloat16 [8192, 384], P(('group', 'view', 'tok')), parts along dimension 0
- values_grad: bfloat16 [8192, 384], P(('group', 'view', 'tok')), parts along dimension 0
- rates_grad: float32 [8192], P(('group', 'view', 'tok')), parts along dimension 0
The draws below stay inside these ranges and needn't reach their ends.
There are 2 independent parts, one for each index of `group`. The reference program is written for one: setup_inputs(seed, part) draws one part's arguments, and reference() takes and returns one part's arrays. A program takes and returns all parts, laid end to end along the dimension named above; an argument that names none is the same for every part. Nothing has to cross between parts.
All inputs are finite; a program needn't handle non-finite values.
Results may differ from the reference program's by a relative error of at most 0.015.
Values may be sent and summed in bfloat16 or wider, within the bound.
A program may use at most 128 MiB of HBM per device.

```python
import math
import jax
import jax.numpy as jnp
from jax import lax

DH = 384
FF = 768
NS_STEPS = 2
TOKENS = 4096


def block_scale(stream_key, extent, shards, low, high):
    loudness, own = 1.0, jax.random.fold_in(stream_key, 6)
    for dim, blocks in shards:
        steps = jnp.exp(jax.random.uniform(jax.random.fold_in(own, dim), (blocks,), jnp.float32, low / len(shards), high / len(shards)))
        loudness = loudness * jnp.repeat(steps, extent[dim] // blocks).reshape([-1 if axis == dim else 1 for axis in range(len(extent))])
    return loudness


def noise(key, dims, deviation, limit, pieces=(), dtype=jnp.bfloat16):
    result = deviation * jax.random.normal(key, dims, jnp.float32)
    if pieces:
        result = result * block_scale(key, dims, pieces, -0.22, 0.18)
    return jnp.clip(result, -limit, limit).astype(dtype)


def setup_inputs(seed: int = 0, part: int = 0) -> dict:
    keys = jax.random.split(jax.random.key(seed), 9)
    own_keys = jax.random.split(jax.random.fold_in(keys[8], part), 9)
    query_rows = noise(own_keys[0], (TOKENS, DH), 1.0, 6.0, ((0, 16),))
    key_rows = noise(own_keys[1], (TOKENS, DH), 1.0, 6.0, ((0, 16),))
    value_rows = noise(own_keys[2], (TOKENS, DH), 1.0, 6.0, ((0, 16),))
    token_rates = jnp.clip(jnp.exp(math.log(4.0) - 2.7725887 * jax.random.uniform(own_keys[3], (TOKENS,), jnp.float32) ** block_scale(own_keys[3], (TOKENS,), ((0, 16),), -0.2, 0.2)), 0.25, 4.0)
    output_cot = noise(own_keys[4], (TOKENS, DH), 1.0, 6.0, ((0, 16),))
    w_gate = noise(keys[5], (FF, DH), DH ** -0.5, 0.3125, (), jnp.float32)
    w_up = noise(keys[6], (FF, DH), DH ** -0.5, 0.3125, (), jnp.float32)
    w_down = noise(keys[7], (FF, DH), FF ** -0.5, 0.21875, (), jnp.float32)
    return {"query_rows": query_rows, "key_rows": key_rows, "value_rows": value_rows, "token_rates": token_rates, "output_cot": output_cot, "w_gate": w_gate, "w_up": w_up, "w_down": w_down}


NS_FIRST = 3.4445
NS_SECOND = -4.775
NS_THIRD = 2.0315
epsilon = 1e-06

def product(left, right):
    return jnp.dot(left, right, preferred_element_type=jnp.float32)

def product_bt(left, right):
    return lax.dot_general(left, right, (((1,), (1,)), ((), ())), preferred_element_type=jnp.float32)

def product_at(left, right):
    return lax.dot_general(left, right, (((0,), (0,)), ((), ())), preferred_element_type=jnp.float32)

def silu_parts(inputs):
    sigmoid_part = jax.nn.sigmoid(inputs)
    activation = inputs * sigmoid_part
    slopes = sigmoid_part * (1.0 + inputs * (1.0 - sigmoid_part))
    curves = sigmoid_part * (1.0 - sigmoid_part) * (2.0 + inputs * (1.0 - 2.0 * sigmoid_part))
    return (activation, slopes, curves)

def key_gradients(key_rows, value_rows, token_rates, gate_half, up_half, down_half):
    key_gate = product_bt(key_rows, gate_half)
    key_up = product_bt(key_rows, up_half)
    activation, slopes, curves = silu_parts(key_gate)
    key_act = (activation * key_up).astype(jnp.bfloat16)
    scaled = (token_rates[:, None] * value_rows.astype(jnp.float32)).astype(jnp.bfloat16)
    key_back = product_bt(scaled, down_half)
    gate_tok = (key_back * key_up * slopes).astype(jnp.bfloat16)
    up_tok = (key_back * activation).astype(jnp.bfloat16)
    partial_grads = (product_at(gate_tok, key_rows), product_at(up_tok, key_rows), product_at(key_act, scaled))
    saved = (key_up, activation, slopes, curves, key_act, scaled, key_back, gate_tok, up_tok)
    return (partial_grads, saved)

def orthogonalize(moment):
    norm_value = jnp.sqrt(jnp.sum(moment * moment) + epsilon)
    current = (moment / norm_value).astype(jnp.bfloat16)
    records = []
    for number in range(NS_STEPS):
        gram_matrix = product_at(current, current).astype(jnp.bfloat16)
        poly_matrix = (NS_SECOND * gram_matrix.astype(jnp.float32) + NS_THIRD * product(gram_matrix, gram_matrix)).astype(jnp.bfloat16)
        records.append((current, gram_matrix, poly_matrix))
        current = (NS_FIRST * current.astype(jnp.float32) + product(current, poly_matrix)).astype(jnp.bfloat16)
    return (current, (moment, norm_value, records))

def orthogonal_backward(record, cotangent):
    moment, norm_value, records = record
    upstream = cotangent
    for current, gram_matrix, poly_matrix in reversed(records):
        upstream_half = upstream.astype(jnp.bfloat16)
        poly_cot = product_at(current, upstream_half)
        poly_cot_half = poly_cot.astype(jnp.bfloat16)
        gram_cot = NS_SECOND * poly_cot + NS_THIRD * (product(poly_cot_half, gram_matrix) + product(gram_matrix, poly_cot_half))
        sym_half = (gram_cot + gram_cot.T).astype(jnp.bfloat16)
        upstream = NS_FIRST * upstream + product_bt(upstream_half, poly_matrix) + product(current, sym_half)
    return upstream / norm_value - moment * (jnp.sum(upstream * moment) / norm_value ** 3)

def query_gradients(query_rows, output_cot, gate_half, up_half, down_half):
    query_gate = product_bt(query_rows, gate_half)
    query_up = product_bt(query_rows, up_half)
    activation, slopes, curves = silu_parts(query_gate)
    query_act = (activation * query_up).astype(jnp.bfloat16)
    query_back = product_bt(output_cot, down_half)
    gate_tok = (query_back * query_up * slopes).astype(jnp.bfloat16)
    up_tok = (query_back * activation).astype(jnp.bfloat16)
    queries_grad = (product(gate_tok, gate_half) + product(up_tok, up_half)).astype(jnp.bfloat16)
    partial_cots = (product_at(gate_tok, query_rows), product_at(up_tok, query_rows), product_at(query_act, output_cot))
    return (queries_grad, partial_cots)

def key_backward(key_rows, value_rows, token_rates, saved, moments, gate_half, up_half, down_half):
    key_up, activation, slopes, curves, key_act, scaled, key_back, gate_tok, up_tok = saved
    mgate_half = moments[0].astype(jnp.bfloat16)
    mup_half = moments[1].astype(jnp.bfloat16)
    mdown_half = moments[2].astype(jnp.bfloat16)
    back_gate = product_bt(key_rows, mgate_half)
    back_up = product_bt(key_rows, mup_half)
    back_act = product_bt(scaled, mdown_half)
    back_keyback = (back_gate * key_up * slopes + back_up * activation).astype(jnp.bfloat16)
    back_keygate = ((back_up * key_back + back_act * key_up) * slopes + back_gate * key_back * key_up * curves).astype(jnp.bfloat16)
    back_keyup = (back_gate * key_back * slopes + back_act * activation).astype(jnp.bfloat16)
    keys_grad = (product(gate_tok, mgate_half) + product(up_tok, mup_half) + product(back_keygate, gate_half) + product(back_keyup, up_half)).astype(jnp.bfloat16)
    values_back = product(key_act, mdown_half) + product(back_keyback, down_half)
    values_grad = (token_rates[:, None] * values_back).astype(jnp.bfloat16)
    rates_grad = lax.optimization_barrier(jnp.sum(value_rows.astype(jnp.float32) * values_back, axis=1))
    return (keys_grad, values_grad, rates_grad)

def reference(query_rows, key_rows, value_rows, token_rates, output_cot, w_gate, w_up, w_down):
    gate_half = w_gate.astype(jnp.bfloat16)
    up_half = w_up.astype(jnp.bfloat16)
    down_half = w_down.astype(jnp.bfloat16)
    partial_grads, saved = key_gradients(key_rows, value_rows, token_rates, gate_half, up_half, down_half)
    results = [orthogonalize(matrix) for matrix in partial_grads]
    new_gate = (w_gate + results[0][0].astype(jnp.float32)).astype(jnp.bfloat16)
    new_up = (w_up + results[1][0].astype(jnp.float32)).astype(jnp.bfloat16)
    new_down = (w_down + results[2][0].astype(jnp.float32)).astype(jnp.bfloat16)
    queries_grad, partial_cots = query_gradients(query_rows, output_cot, new_gate, new_up, new_down)
    moments = [orthogonal_backward(results[index][1], partial_cots[index]) for index in range(3)]
    keys_grad, values_grad, rates_grad = key_backward(key_rows, value_rows, token_rates, saved, moments, gate_half, up_half, down_half)
    return (queries_grad, keys_grad, values_grad, rates_grad)
```

```python
import functools

import jax
import jax.numpy as jnp
from jax import lax
from jax.experimental import pallas as pl
from jax.experimental.pallas import tpu as pltpu
from jax.sharding import PartitionSpec as P

NS_STEPS = 2
NS_FIRST = 3.4445
NS_SECOND = -4.775
NS_THIRD = 2.0315
EPSILON = 1e-06
MESH = pl.DeviceIdType.MESH
BF = jnp.bfloat16
F32 = jnp.float32
GATE, UP, DOWN = 0, 1, 2
HALVINGS = 3


def dot(left, right):
    return jnp.dot(left, right, preferred_element_type=F32)


def dot_bt(left, right):
    return lax.dot_general(left, right, (((1,), (1,)), ((), ())), preferred_element_type=F32)


def total_of(values):
    return jnp.sum(jnp.sum(values, axis=1, keepdims=True), axis=0, keepdims=True)


def bits_of(axis, size):
    bits, bit = [], 1
    while bit < size:
        bits.append((axis, bit))
        bit *= 2
    return bits


class Summing:
    def __init__(self, orders, acc, res, halved, exchanged, between, send_sem, recv_sem, number, matrix, half):
        self.order = orders[half]
        self.where = (number, matrix, half)
        self.acc, self.res = acc.at[number, matrix, half], res.at[number, matrix, half]
        self.halved = [ref.at[number, matrix, half] for ref in halved]
        self.exchanged = [ref.at[number, matrix, half] for ref in exchanged]
        self.between = [ref.at[number, matrix, half] for ref in between]
        self.send_sem, self.recv_sem = send_sem, recv_sem
        self.extent = acc.shape[-2]
        self.offset, self.size = 0, self.extent
        self.levels = len(self.order)
        self.halvings = min(HALVINGS, self.levels - 1)
        self.offsets = []
        self.step = 0
        self.pending, self.sent = None, []

    def side(self, level):
        axis, bit = self.order[level]
        place = lax.axis_index(axis)
        mine = lax.rem(place // bit, 2)
        return mine, {axis: place + bit * (1 - 2 * mine)}

    def rows(self, offset, size):
        if isinstance(offset, int):
            return pl.ds(offset, size)
        return pl.ds(pl.multiple_of(offset, 16), size)

    def send(self, source, target, device):
        slot = self.where + (self.step,)
        copy = pltpu.make_async_remote_copy(
            src_ref=source,
            dst_ref=target,
            send_sem=self.send_sem.at[slot],
            recv_sem=self.recv_sem.at[slot],
            device_id=device,
            device_id_type=MESH,
        )
        copy.start()
        self.pending = copy
        self.sent.append(copy)

    def advance(self):
        step, halvings, levels = self.step, self.halvings, self.levels
        if step > 0:
            self.pending.wait_recv()
            last = step - 1
            if last < halvings:
                here = self.rows(self.offset, self.size)
                self.acc[here, :] = (
                    self.acc[here, :].astype(F32) + self.halved[last][...].astype(F32)
                ).astype(BF)
            elif last < levels:
                place = last - halvings
                if place == 0:
                    own = self.acc[self.rows(self.offset, self.size), :]
                else:
                    own = self.between[place - 1][...]
                summed = (own.astype(F32) + self.exchanged[place][...].astype(F32)).astype(BF)
                if last == levels - 1:
                    self.res[self.rows(self.offset, self.size), :] = summed
                else:
                    self.between[place][...] = summed
            else:
                back = halvings - 1 - (last - levels)
                self.offset, self.size = self.offsets[back], self.size * 2
        if step < halvings:
            mine, device = self.side(step)
            size = self.size // 2
            self.offsets.append(self.offset)
            self.send(self.acc.at[self.rows(self.offset + (1 - mine) * size, size), :], self.halved[step], device)
            self.offset, self.size = self.offset + mine * size, size
        elif step < levels:
            place = step - halvings
            _, device = self.side(step)
            source = self.acc.at[self.rows(self.offset, self.size), :] if place == 0 else self.between[place - 1]
            self.send(source, self.exchanged[place], device)
        elif step < levels + halvings:
            _, device = self.side(halvings - 1 - (step - levels))
            here = self.rows(self.offset, self.size)
            self.send(self.res.at[here, :], self.res.at[here, :], device)
        self.step += 1

    @property
    def steps(self):
        return self.levels + self.halvings


def kernel(
    orders, n_halved, n_exchanged,
    q_ref, k_ref, v_ref, r_ref, o_ref, wg_ref, wu_ref, wd_ref,
    dq_ref, dk_ref, dv_ref, dr_ref,
    acc, res, xs, grams, polys, new_t, w_t, saved, toks, send_sem, recv_sem, *levels,
):
    halved, exchanged = levels[:n_halved], levels[n_halved:n_halved + n_exchanged]
    between = levels[n_halved + n_exchanged:]
    width = acc.shape[-1]
    halves = new_t.shape[-1] // width

    barrier = pltpu.get_barrier_semaphore()
    for axis, bit in orders[0]:
        place = lax.axis_index(axis)
        peer = place + bit * (1 - 2 * lax.rem(place // bit, 2))
        pl.semaphore_signal(barrier, inc=1, device_id={axis: peer}, device_id_type=MESH)

    chunks = {}
    every = []

    def begin(number, matrix, values):
        for half in range(halves):
            acc[number, matrix, half] = values[:, half * width:(half + 1) * width].astype(BF)
            chunk = Summing(
                orders, acc, res, halved, exchanged, between, send_sem, recv_sem, number, matrix, half
            )
            chunk.advance()
            chunks[number, matrix, half] = chunk
            every.append(chunk)

    def pump(number, matrix):
        for half in range(halves):
            chunk = chunks[number, matrix, half]
            if chunk.step <= chunk.steps:
                chunk.advance()

    def total(number, matrix):
        return jnp.concatenate([res[number, matrix, half] for half in range(halves)], axis=1)

    k = k_ref[...]
    k_t = k.T
    key_gate = dot_bt(k, wg_ref[...].astype(BF))
    key_up = dot_bt(k, wu_ref[...].astype(BF))
    sig = jax.nn.sigmoid(key_gate)
    act = key_gate * sig
    slopes = sig * (1.0 + key_gate * (1.0 - sig))
    toks[DOWN] = (act * key_up).astype(BF)
    scaled = (r_ref[...] * v_ref[...].astype(F32)).astype(BF)
    down_grad = dot(scaled.T, toks[DOWN])
    pl.semaphore_wait(barrier, len(orders[0]))
    begin(0, DOWN, down_grad)
    key_back = dot_bt(scaled, wd_ref[...].astype(BF))
    toks[UP] = (key_back * act).astype(BF)
    begin(0, UP, dot(k_t, toks[UP]))
    toks[GATE] = (key_back * key_up * slopes).astype(BF)
    begin(0, GATE, dot(k_t, toks[GATE]))
    pump(0, DOWN)
    curves = sig * (1.0 - sig) * (2.0 + key_gate * (1.0 - 2.0 * sig))
    saved[0] = act
    saved[1] = key_up * slopes
    pump(0, UP)
    pump(0, DOWN)
    saved[2] = key_back * slopes
    saved[3] = key_back * key_up * curves
    pump(0, GATE)
    pump(0, UP)
    pump(0, DOWN)
    w_t[DOWN] = wd_ref[...].T
    pump(0, GATE)
    pump(0, UP)
    pump(0, DOWN)
    w_t[UP] = wu_ref[...].T
    pump(0, GATE)
    pump(0, UP)
    pump(0, DOWN)
    w_t[GATE] = wg_ref[...].T

    inverse = {}

    def ortho_start(matrix):
        moment = total(0, matrix).astype(F32)
        inverse[matrix] = 1.0 / jnp.sqrt(total_of(moment * moment) + EPSILON)
        xs[matrix, 0] = (moment * inverse[matrix]).astype(BF)

    def ortho_step(matrix, number):
        current = xs[matrix, number]
        gram = dot_bt(current, current).astype(BF)
        poly = (NS_SECOND * gram.astype(F32) + NS_THIRD * dot(gram, gram)).astype(BF)
        grams[matrix, number] = gram
        polys[matrix, number] = poly
        following = (NS_FIRST * current.astype(F32) + dot(poly, current)).astype(BF)
        if number + 1 < NS_STEPS:
            xs[matrix, number + 1] = following
        else:
            new_t[matrix] = (w_t[matrix] + following.astype(F32)).astype(BF)

    def ortho(matrix, others):
        ortho_start(matrix)
        for number in range(NS_STEPS):
            for other in others:
                pump(0, other)
            ortho_step(matrix, number)

    def finish(number, matrix):
        while chunks[number, matrix, 0].step <= chunks[number, matrix, 0].steps:
            pump(number, matrix)

    pump(0, GATE)
    pump(0, UP)
    pump(0, DOWN)
    pump(0, GATE)
    pump(0, UP)
    finish(0, DOWN)
    pump(0, GATE)
    pump(0, UP)
    ortho(DOWN, (GATE, UP))
    finish(0, UP)
    query_back = dot(o_ref[...], new_t[DOWN])
    ortho(UP, (GATE,))
    finish(0, GATE)
    q = q_ref[...]
    query_up = dot(q, new_t[UP])
    q_t = q.T
    o_t = o_ref[...].T
    ortho(GATE, ())

    query_gate = dot(q, new_t[GATE])
    sig = jax.nn.sigmoid(query_gate)
    act = query_gate * sig
    slopes = sig * (1.0 + query_gate * (1.0 - sig))
    begin(1, DOWN, dot(o_t, (act * query_up).astype(BF)))
    qup_tok = (query_back * act).astype(BF)
    begin(1, UP, dot(q_t, qup_tok))
    qgate_tok = (query_back * query_up * slopes).astype(BF)
    begin(1, GATE, dot(q_t, qgate_tok))
    pump(1, DOWN)
    pump(1, UP)
    queries = dot_bt(qup_tok, new_t[UP])
    pump(1, DOWN)
    pump(1, GATE)
    pump(1, UP)
    pump(1, DOWN)
    dq_ref[...] = (queries + dot_bt(qgate_tok, new_t[GATE])).astype(BF)
    for _ in range(3):
        pump(1, GATE)
        pump(1, UP)
        pump(1, DOWN)

    def unortho(matrix, others):
        upstream_half = total(1, matrix)
        upstream = upstream_half.astype(F32)
        for number in reversed(range(NS_STEPS)):
            for other in others:
                pump(1, other)
            current = xs[matrix, number]
            poly_cot = dot_bt(current, upstream_half)
            poly_cot = poly_cot + poly_cot.T
            mixed = dot(poly_cot.astype(BF), grams[matrix, number])
            sym = (NS_SECOND * poly_cot + NS_THIRD * (mixed + mixed.T)).astype(BF)
            upstream = NS_FIRST * upstream + dot(
                jnp.concatenate([polys[matrix, number], sym], axis=1),
                jnp.concatenate([upstream_half, current], axis=0),
            )
            upstream_half = upstream.astype(BF)
        moment = total(0, matrix).astype(F32)
        inv = inverse[matrix]
        return (upstream * inv - moment * (total_of(upstream * moment) * (inv * inv * inv))).astype(BF)

    pump(1, GATE)
    pump(1, UP)
    finish(1, DOWN)
    mdown = unortho(DOWN, (GATE, UP))
    finish(1, UP)
    scaled = (r_ref[...] * v_ref[...].astype(F32)).astype(BF)
    back_act = dot(scaled, mdown)
    values = dot_bt(toks[DOWN], mdown)
    mup = unortho(UP, (GATE,))
    finish(1, GATE)
    k = k_ref[...]
    back_up = dot(k, mup)
    keys = dot_bt(toks[UP], mup)
    mgate = unortho(GATE, ())
    back_gate = dot(k, mgate)
    back_keyback = (back_gate * saved[1] + back_up * saved[0]).astype(BF)
    values = values + dot(back_keyback, wd_ref[...].astype(BF))
    dv_ref[...] = (r_ref[...] * values).astype(BF)
    dr_ref[...] = jnp.sum(v_ref[...].astype(F32) * values, axis=1, keepdims=True)
    back_keygate = (back_up * saved[2] + back_act * saved[1] + back_gate * saved[3]).astype(BF)
    back_keyup = (back_gate * saved[2] + back_act * saved[0]).astype(BF)
    keys = keys + dot_bt(toks[GATE], mgate)
    keys = keys + dot(back_keygate, wg_ref[...].astype(BF)) + dot(back_keyup, wu_ref[...].astype(BF))
    dk_ref[...] = keys.astype(BF)
    for chunk in every:
        for copy in chunk.sent:
            copy.wait_send()


def on_device(n_view, n_tok, q, k, v, r, o, wg, wu, wd):
    rows, features = q.shape
    hidden = wg.shape[0]
    tok_bits, view_bits = bits_of("tok", n_tok), bits_of("view", n_view)
    orders = (tok_bits + view_bits, tok_bits[:1] + view_bits + tok_bits[1:])
    levels = len(orders[0])
    n_halved = min(HALVINGS, levels - 1)
    n_exchanged = levels - n_halved
    width = hidden // 2
    segment = features >> n_halved
    lead = (2, 3, 2)
    vmem = pl.BlockSpec(memory_space=pltpu.VMEM)
    steps = levels + n_halved
    outs = pl.pallas_call(
        functools.partial(kernel, orders, n_halved, n_exchanged),
        out_shape=(
            jax.ShapeDtypeStruct((rows, features), BF),
            jax.ShapeDtypeStruct((rows, features), BF),
            jax.ShapeDtypeStruct((rows, features), BF),
            jax.ShapeDtypeStruct((rows, 1), F32),
        ),
        in_specs=[vmem] * 8,
        out_specs=(vmem,) * 4,
        scratch_shapes=[
            pltpu.VMEM(lead + (features, width), BF),
            pltpu.VMEM(lead + (features, width), BF),
            pltpu.VMEM((3, NS_STEPS, features, hidden), BF),
            pltpu.VMEM((3, NS_STEPS, features, features), BF),
            pltpu.VMEM((3, NS_STEPS, features, features), BF),
            pltpu.VMEM((3, features, hidden), BF),
            pltpu.VMEM((3, features, hidden), F32),
            pltpu.VMEM((4, rows, hidden), F32),
            pltpu.VMEM((3, rows, hidden), BF),
            pltpu.SemaphoreType.DMA(lead + (steps,)),
            pltpu.SemaphoreType.DMA(lead + (steps,)),
        ]
        + [pltpu.VMEM(lead + (features >> (level + 1), width), BF) for level in range(n_halved)]
        + [pltpu.VMEM(lead + (segment, width), BF) for _ in range(n_exchanged)]
        + [pltpu.VMEM(lead + (segment, width), BF) for _ in range(n_exchanged - 1)],
        compiler_params=pltpu.CompilerParams(
            collective_id=0, has_side_effects=True, vmem_limit_bytes=60 * 1024 * 1024
        ),
    )(q, k, v, r.reshape(rows, 1), o, wg, wu, wd)
    return (outs[0], outs[1], outs[2], outs[3].reshape(rows))


def solution(mesh):
    rows = P(("group", "view", "tok"), None)
    flat = P(("group", "view", "tok"))
    return jax.shard_map(
        functools.partial(on_device, mesh.shape["view"], mesh.shape["tok"]),
        mesh=mesh,
        in_specs=(rows, rows, rows, flat, rows, P(), P(), P()),
        out_specs=(rows, rows, rows, flat),
        check_vma=False,
    )
```

```python
import functools

import jax
import jax.numpy as jnp
from jax import lax
from jax.experimental import pallas as pl
from jax.experimental.pallas import tpu as pltpu
from jax.sharding import PartitionSpec as P

NS_STEPS = 2
NS_FIRST = 3.4445
NS_SECOND = -4.775
NS_THIRD = 2.0315
EPSILON = 1e-06
MESH = pl.DeviceIdType.MESH
BF = jnp.bfloat16
F32 = jnp.float32
GATE, UP, DOWN = 0, 1, 2
HALVINGS = 3


def dot(left, right):
    return jnp.dot(left, right, preferred_element_type=F32)


def dot_bt(left, right):
    return lax.dot_general(left, right, (((1,), (1,)), ((), ())), preferred_element_type=F32)


def total_of(values):
    return jnp.sum(jnp.sum(values, axis=1, keepdims=True), axis=0, keepdims=True)


def bits_of(axis, size):
    bits, bit = [], 1
    while bit < size:
        bits.append((axis, bit))
        bit *= 2
    return bits


class Summing:
    def __init__(self, orders, acc, res, halved, exchanged, between, send_sem, recv_sem, number, matrix, half):
        self.order = orders[half]
        self.where = (number, matrix, half)
        self.acc, self.res = acc.at[number, matrix, half], res.at[number, matrix, half]
        self.halved = [ref.at[number, matrix, half] for ref in halved]
        self.exchanged = [ref.at[number, matrix, half] for ref in exchanged]
        self.between = [ref.at[number, matrix, half] for ref in between]
        self.send_sem, self.recv_sem = send_sem, recv_sem
        self.extent = acc.shape[-2]
        self.offset, self.size = 0, self.extent
        self.levels = len(self.order)
        self.halvings = min(HALVINGS, self.levels - 1)
        self.offsets = []
        self.step = 0
        self.pending, self.sent = None, []

    def side(self, level):
        axis, bit = self.order[level]
        place = lax.axis_index(axis)
        mine = lax.rem(place // bit, 2)
        return mine, {axis: place + bit * (1 - 2 * mine)}

    def rows(self, offset, size):
        if isinstance(offset, int):
            return pl.ds(offset, size)
        return pl.ds(pl.multiple_of(offset, 16), size)

    def send(self, source, target, device):
        slot = self.where + (self.step,)
        copy = pltpu.make_async_remote_copy(
            src_ref=source,
            dst_ref=target,
            send_sem=self.send_sem.at[slot],
            recv_sem=self.recv_sem.at[slot],
            device_id=device,
            device_id_type=MESH,
        )
        copy.start()
        self.pending = copy
        self.sent.append(copy)

    def advance(self):
        step, halvings, levels = self.step, self.halvings, self.levels
        if step > 0:
            self.pending.wait_recv()
            last = step - 1
            if last < halvings:
                here = self.rows(self.offset, self.size)
                self.acc[here, :] = (
                    self.acc[here, :].astype(F32) + self.halved[last][...].astype(F32)
                ).astype(BF)
            elif last < levels:
                place = last - halvings
                if place == 0:
                    own = self.acc[self.rows(self.offset, self.size), :]
                else:
                    own = self.between[place - 1][...]
                summed = (own.astype(F32) + self.exchanged[place][...].astype(F32)).astype(BF)
                if last == levels - 1:
                    self.res[self.rows(self.offset, self.size), :] = summed
                else:
                    self.between[place][...] = summed
            else:
                back = halvings - 1 - (last - levels)
                self.offset, self.size = self.offsets[back], self.size * 2
        if step < halvings:
            mine, device = self.side(step)
            size = self.size // 2
            self.offsets.append(self.offset)
            self.send(self.acc.at[self.rows(self.offset + (1 - mine) * size, size), :], self.halved[step], device)
            self.offset, self.size = self.offset + mine * size, size
        elif step < levels:
            place = step - halvings
            _, device = self.side(step)
            source = self.acc.at[self.rows(self.offset, self.size), :] if place == 0 else self.between[place - 1]
            self.send(source, self.exchanged[place], device)
        elif step < levels + halvings:
            _, device = self.side(halvings - 1 - (step - levels))
            here = self.rows(self.offset, self.size)
            self.send(self.res.at[here, :], self.res.at[here, :], device)
        self.step += 1

    @property
    def steps(self):
        return self.levels + self.halvings


def kernel(
    orders, n_halved, n_exchanged,
    q_ref, k_ref, v_ref, r_ref, o_ref, wg_ref, wu_ref, wd_ref,
    dq_ref, dk_ref, dv_ref, dr_ref,
    acc, res, xs, grams, polys, new_t, w_t, saved, toks, send_sem, recv_sem, *levels,
):
    halved, exchanged = levels[:n_halved], levels[n_halved:n_halved + n_exchanged]
    between = levels[n_halved + n_exchanged:]
    width = acc.shape[-1]
    halves = new_t.shape[-1] // width

    barrier = pltpu.get_barrier_semaphore()
    for axis, bit in orders[0]:
        place = lax.axis_index(axis)
        peer = place + bit * (1 - 2 * lax.rem(place // bit, 2))
        pl.semaphore_signal(barrier, inc=1, device_id={axis: peer}, device_id_type=MESH)

    chunks = {}
    every = []

    def begin(number, matrix, values):
        for half in range(halves):
            acc[number, matrix, half] = values[:, half * width:(half + 1) * width].astype(BF)
            chunk = Summing(
                orders, acc, res, halved, exchanged, between, send_sem, recv_sem, number, matrix, half
            )
            chunk.advance()
            chunks[number, matrix, half] = chunk
            every.append(chunk)

    def pump(number, matrix):
        for half in range(halves):
            chunk = chunks[number, matrix, half]
            if chunk.step <= chunk.steps:
                chunk.advance()

    def finish(number, matrix):
        while chunks[number, matrix, 0].step <= chunks[number, matrix, 0].steps:
            pump(number, matrix)

    def total(number, matrix):
        finish(number, matrix)
        return jnp.concatenate([res[number, matrix, half] for half in range(halves)], axis=1)

    rates = jnp.broadcast_to(r_ref[...], (8, r_ref.shape[1])).T[:, :1]
    k = k_ref[...]
    k_t = k.T
    key_gate = dot_bt(k, wg_ref[...].astype(BF))
    key_up = dot_bt(k, wu_ref[...].astype(BF))
    sig = jax.nn.sigmoid(key_gate)
    act = key_gate * sig
    slopes = sig * (1.0 + key_gate * (1.0 - sig))
    toks[DOWN] = (act * key_up).astype(BF)
    scaled = (rates * v_ref[...].astype(F32)).astype(BF)
    down_grad = dot(scaled.T, toks[DOWN])
    pl.semaphore_wait(barrier, len(orders[0]))
    begin(0, DOWN, down_grad)
    key_back = dot_bt(scaled, wd_ref[...].astype(BF))
    toks[UP] = (key_back * act).astype(BF)
    begin(0, UP, dot(k_t, toks[UP]))
    toks[GATE] = (key_back * key_up * slopes).astype(BF)
    begin(0, GATE, dot(k_t, toks[GATE]))
    pump(0, DOWN)
    curves = sig * (1.0 - sig) * (2.0 + key_gate * (1.0 - 2.0 * sig))
    saved[0] = act
    saved[1] = key_up * slopes
    pump(0, UP)
    pump(0, DOWN)
    saved[2] = key_back * slopes
    saved[3] = key_back * key_up * curves
    pump(0, GATE)
    pump(0, UP)
    pump(0, DOWN)
    w_t[DOWN] = wd_ref[...].T
    pump(0, GATE)
    pump(0, UP)
    pump(0, DOWN)
    w_t[UP] = wu_ref[...].T
    pump(0, GATE)
    pump(0, UP)
    pump(0, DOWN)
    w_t[GATE] = wg_ref[...].T

    inverse = {}

    def ortho_start(matrix):
        moment = total(0, matrix).astype(F32)
        inverse[matrix] = 1.0 / jnp.sqrt(total_of(moment * moment) + EPSILON)
        xs[matrix, 0] = (moment * inverse[matrix]).astype(BF)

    def ortho_step(matrix, number):
        current = xs[matrix, number]
        gram = dot_bt(current, current).astype(BF)
        poly = (NS_SECOND * gram.astype(F32) + NS_THIRD * dot(gram, gram)).astype(BF)
        grams[matrix, number] = gram
        polys[matrix, number] = poly
        following = (NS_FIRST * current.astype(F32) + dot(poly, current)).astype(BF)
        if number + 1 < NS_STEPS:
            xs[matrix, number + 1] = following
        else:
            new_t[matrix] = (w_t[matrix] + following.astype(F32)).astype(BF)

    def ortho(matrix):
        ortho_start(matrix)
        for number in range(NS_STEPS):
            ortho_step(matrix, number)

    def tick(number, *matrices):
        for matrix in matrices:
            pump(number, matrix)

    tick(0, GATE, UP, DOWN)
    q = q_ref[...]
    q_t = q.T
    o_t = o_ref[...].T
    tick(0, GATE, UP, DOWN)
    ortho(DOWN)
    tick(0, GATE, UP)
    query_back = dot(o_ref[...], new_t[DOWN])
    ortho(UP)
    tick(0, GATE)
    query_up = dot(q, new_t[UP])
    ortho(GATE)

    query_gate = dot(q, new_t[GATE])
    sig = jax.nn.sigmoid(query_gate)
    act = query_gate * sig
    slopes = sig * (1.0 + query_gate * (1.0 - sig))
    begin(1, DOWN, dot(o_t, (act * query_up).astype(BF)))
    qgate_tok = (query_back * query_up * slopes).astype(BF)
    begin(1, GATE, dot(q_t, qgate_tok))
    tick(1, DOWN)
    qup_tok = (query_back * act).astype(BF)
    begin(1, UP, dot(q_t, qup_tok))
    tick(1, GATE, DOWN)
    queries = dot_bt(qup_tok, new_t[UP])
    tick(1, UP, GATE, DOWN)
    dq_ref[...] = (queries + dot_bt(qgate_tok, new_t[GATE])).astype(BF)
    tick(1, UP, GATE, DOWN)
    scaled = (rates * v_ref[...].astype(F32)).astype(BF)
    k = k_ref[...]
    for _ in range(3):
        tick(1, UP, GATE, DOWN)

    def unortho(matrix):
        upstream_half = total(1, matrix)
        upstream = upstream_half.astype(F32)
        for number in reversed(range(NS_STEPS)):
            current = xs[matrix, number]
            poly_cot = dot_bt(current, upstream_half)
            poly_cot = poly_cot + poly_cot.T
            mixed = dot(poly_cot.astype(BF), grams[matrix, number])
            sym = (NS_SECOND * poly_cot + NS_THIRD * (mixed + mixed.T)).astype(BF)
            upstream = NS_FIRST * upstream + dot(
                jnp.concatenate([polys[matrix, number], sym], axis=1),
                jnp.concatenate([upstream_half, current], axis=0),
            )
            upstream_half = upstream.astype(BF)
        moment = total(0, matrix).astype(F32)
        inv = inverse[matrix]
        return (upstream * inv - moment * (total_of(upstream * moment) * (inv * inv * inv))).astype(BF)

    mdown = unortho(DOWN)
    tick(1, UP, GATE)
    back_act = dot(scaled, mdown)
    values = dot_bt(toks[DOWN], mdown)
    mgate = unortho(GATE)
    tick(1, UP)
    back_gate = dot(k, mgate)
    keys = dot_bt(toks[GATE], mgate)
    back_keyup = (back_gate * saved[2] + back_act * saved[0]).astype(BF)
    keys = keys + dot(back_keyup, wu_ref[...].astype(BF))
    keygate_part = back_act * saved[1] + back_gate * saved[3]
    keyback_part = back_gate * saved[1]
    mup = unortho(UP)
    back_up = dot(k, mup)
    back_keyback = (keyback_part + back_up * saved[0]).astype(BF)
    values = values + dot(back_keyback, wd_ref[...].astype(BF))
    dv_ref[...] = (rates * values).astype(BF)
    rates_grad = jnp.sum(v_ref[...].astype(F32) * values, axis=1, keepdims=True)
    dr_ref[...] = jnp.broadcast_to(rates_grad, (rates_grad.shape[0], 128)).T[:1]
    back_keygate = (keygate_part + back_up * saved[2]).astype(BF)
    keys = keys + dot_bt(toks[UP], mup) + dot(back_keygate, wg_ref[...].astype(BF))
    dk_ref[...] = keys.astype(BF)
    for chunk in every:
        for copy in chunk.sent:
            copy.wait_send()


def handing(*refs):
    for source, target in zip(refs[:4], refs[4:]):
        target[...] = source[...]


def on_device(n_view, n_tok, q, k, v, r, o, wg, wu, wd):
    rows, features = q.shape
    hidden = wg.shape[0]
    tok_bits, view_bits = bits_of("tok", n_tok), bits_of("view", n_view)
    orders = (tok_bits + view_bits, tok_bits[:1] + view_bits[:1] + tok_bits[1:] + view_bits[1:])
    levels = len(orders[0])
    n_halved = min(HALVINGS, levels - 1)
    n_exchanged = levels - n_halved
    width = hidden // 2
    segment = features >> n_halved
    lead = (2, 3, 2)
    vmem = pl.BlockSpec(memory_space=pltpu.VMEM)
    steps = levels + n_halved
    outs = pl.pallas_call(
        functools.partial(kernel, orders, n_halved, n_exchanged),
        out_shape=(
            jax.ShapeDtypeStruct((rows, features), BF),
            jax.ShapeDtypeStruct((rows, features), BF),
            jax.ShapeDtypeStruct((rows, features), BF),
            jax.ShapeDtypeStruct((1, rows), F32),
        ),
        in_specs=[vmem] * 8,
        out_specs=(vmem,) * 4,
        scratch_shapes=[
            pltpu.VMEM(lead + (features, width), BF),
            pltpu.VMEM(lead + (features, width), BF),
            pltpu.VMEM((3, NS_STEPS, features, hidden), BF),
            pltpu.VMEM((3, NS_STEPS, features, features), BF),
            pltpu.VMEM((3, NS_STEPS, features, features), BF),
            pltpu.VMEM((3, features, hidden), BF),
            pltpu.VMEM((3, features, hidden), F32),
            pltpu.VMEM((4, rows, hidden), F32),
            pltpu.VMEM((3, rows, hidden), BF),
            pltpu.SemaphoreType.DMA(lead + (steps,)),
            pltpu.SemaphoreType.DMA(lead + (steps,)),
        ]
        + [pltpu.VMEM(lead + (features >> (level + 1), width), BF) for level in range(n_halved)]
        + [pltpu.VMEM(lead + (segment, width), BF) for _ in range(n_exchanged)]
        + [pltpu.VMEM(lead + (segment, width), BF) for _ in range(n_exchanged - 1)],
        compiler_params=pltpu.CompilerParams(
            collective_id=0, has_side_effects=True, vmem_limit_bytes=60 * 1024 * 1024
        ),
    )(q, k, v, r.reshape(1, rows), o, wg, wu, wd)
    outs = pl.pallas_call(
        handing,
        out_shape=tuple(jax.ShapeDtypeStruct(out.shape, out.dtype) for out in outs),
        in_specs=[vmem] * 4,
        out_specs=(vmem,) * 4,
    )(*outs)
    return (outs[0], outs[1], outs[2], outs[3].reshape(rows))


def solution(mesh):
    rows = P(("group", "view", "tok"), None)
    flat = P(("group", "view", "tok"))
    return jax.shard_map(
        functools.partial(on_device, mesh.shape["view"], mesh.shape["tok"]),
        mesh=mesh,
        in_specs=(rows, rows, rows, flat, rows, P(), P(), P()),
        out_specs=(rows, rows, rows, flat),
        check_vma=False,
    )
```

```python
import functools

import jax
import jax.numpy as jnp
from jax import lax
from jax.experimental import pallas as pl
from jax.experimental.pallas import tpu as pltpu
from jax.sharding import PartitionSpec as P

NS_STEPS = 2
NS_FIRST = 3.4445
NS_SECOND = -4.775
NS_THIRD = 2.0315
EPSILON = 1e-06
MESH = pl.DeviceIdType.MESH
BF = jnp.bfloat16
F32 = jnp.float32
GATE, UP, DOWN = 0, 1, 2
HALVINGS = 3


def dot(left, right):
    return jnp.dot(left, right, preferred_element_type=F32)


def dot_bt(left, right):
    return lax.dot_general(left, right, (((1,), (1,)), ((), ())), preferred_element_type=F32)


def total_of(values):
    return jnp.sum(jnp.sum(values, axis=1, keepdims=True), axis=0, keepdims=True)


def bits_of(axis, size):
    bits, bit = [], 1
    while bit < size:
        bits.append((axis, bit))
        bit *= 2
    return bits


class Summing:
    def __init__(self, orders, acc, res, halved, exchanged, between, send_sem, recv_sem, number, matrix, half):
        self.order = orders[half]
        self.where = (number, matrix, half)
        self.acc, self.res = acc.at[number, matrix, half], res.at[number, matrix, half]
        self.halved = [ref.at[number, matrix, half] for ref in halved]
        self.exchanged = [ref.at[number, matrix, half] for ref in exchanged]
        self.between = [ref.at[number, matrix, half] for ref in between]
        self.send_sem, self.recv_sem = send_sem, recv_sem
        self.extent = acc.shape[-2]
        self.offset, self.size = 0, self.extent
        self.levels = len(self.order)
        self.halvings = min(HALVINGS, self.levels - 1)
        self.offsets = []
        self.step = 0
        self.pending, self.sent = None, []

    def side(self, level):
        axis, bit = self.order[level]
        place = lax.axis_index(axis)
        mine = lax.rem(place // bit, 2)
        return mine, {axis: place + bit * (1 - 2 * mine)}

    def rows(self, offset, size):
        if isinstance(offset, int):
            return pl.ds(offset, size)
        return pl.ds(pl.multiple_of(offset, 16), size)

    def send(self, source, target, device):
        slot = self.where + (self.step,)
        copy = pltpu.make_async_remote_copy(
            src_ref=source,
            dst_ref=target,
            send_sem=self.send_sem.at[slot],
            recv_sem=self.recv_sem.at[slot],
            device_id=device,
            device_id_type=MESH,
        )
        copy.start()
        self.pending = copy
        self.sent.append(copy)

    def advance(self):
        step, halvings, levels = self.step, self.halvings, self.levels
        if step > 0:
            self.pending.wait_recv()
            last = step - 1
            if last < halvings:
                here = self.rows(self.offset, self.size)
                self.acc[here, :] = (
                    self.acc[here, :].astype(F32) + self.halved[last][...].astype(F32)
                ).astype(BF)
            elif last < levels:
                place = last - halvings
                if place == 0:
                    own = self.acc[self.rows(self.offset, self.size), :]
                else:
                    own = self.between[place - 1][...]
                summed = (own.astype(F32) + self.exchanged[place][...].astype(F32)).astype(BF)
                if last == levels - 1:
                    self.res[self.rows(self.offset, self.size), :] = summed
                else:
                    self.between[place][...] = summed
            else:
                back = halvings - 1 - (last - levels)
                self.offset, self.size = self.offsets[back], self.size * 2
        if step < halvings:
            mine, device = self.side(step)
            size = self.size // 2
            self.offsets.append(self.offset)
            self.send(self.acc.at[self.rows(self.offset + (1 - mine) * size, size), :], self.halved[step], device)
            self.offset, self.size = self.offset + mine * size, size
        elif step < levels:
            place = step - halvings
            _, device = self.side(step)
            source = self.acc.at[self.rows(self.offset, self.size), :] if place == 0 else self.between[place - 1]
            self.send(source, self.exchanged[place], device)
        elif step < levels + halvings:
            _, device = self.side(halvings - 1 - (step - levels))
            here = self.rows(self.offset, self.size)
            self.send(self.res.at[here, :], self.res.at[here, :], device)
        self.step += 1

    @property
    def steps(self):
        return self.levels + self.halvings


def kernel(
    orders, n_halved, n_exchanged,
    q_ref, k_ref, v_ref, r_ref, o_ref, wg_ref, wu_ref, wd_ref,
    dq_ref, dk_ref, dv_ref, dr_ref,
    acc, res, xs, grams, polys, new_t, w_t, saved, toks, send_sem, recv_sem, *levels,
):
    halved, exchanged = levels[:n_halved], levels[n_halved:n_halved + n_exchanged]
    between = levels[n_halved + n_exchanged:]
    width = acc.shape[-1]
    halves = new_t.shape[-1] // width

    barrier = pltpu.get_barrier_semaphore()
    for axis, bit in orders[0]:
        place = lax.axis_index(axis)
        peer = place + bit * (1 - 2 * lax.rem(place // bit, 2))
        pl.semaphore_signal(barrier, inc=1, device_id={axis: peer}, device_id_type=MESH)

    chunks = {}
    every = []

    def begin(number, matrix, values):
        for half in range(halves):
            acc[number, matrix, half] = values[:, half * width:(half + 1) * width].astype(BF)
            chunk = Summing(
                orders, acc, res, halved, exchanged, between, send_sem, recv_sem, number, matrix, half
            )
            chunk.advance()
            chunks[number, matrix, half] = chunk
            every.append(chunk)

    def pump(number, matrix):
        for half in reversed(range(halves)):
            chunk = chunks[number, matrix, half]
            if chunk.step <= chunk.steps:
                chunk.advance()

    def finish(number, matrix):
        while chunks[number, matrix, 0].step <= chunks[number, matrix, 0].steps:
            pump(number, matrix)

    def total(number, matrix):
        finish(number, matrix)
        return jnp.concatenate([res[number, matrix, half] for half in range(halves)], axis=1)

    rates = jnp.broadcast_to(r_ref[...], (8, r_ref.shape[1])).T[:, :1]
    k = k_ref[...]
    k_t = k.T
    key_gate = dot_bt(k, wg_ref[...].astype(BF))
    key_up = dot_bt(k, wu_ref[...].astype(BF))
    sig = jax.nn.sigmoid(key_gate)
    act = key_gate * sig
    slopes = sig * (1.0 + key_gate * (1.0 - sig))
    toks[DOWN] = (act * key_up).astype(BF)
    scaled = (rates * v_ref[...].astype(F32)).astype(BF)
    down_grad = dot(scaled.T, toks[DOWN])
    pl.semaphore_wait(barrier, len(orders[0]))
    begin(0, DOWN, down_grad)
    key_back = dot_bt(scaled, wd_ref[...].astype(BF))
    toks[UP] = (key_back * act).astype(BF)
    begin(0, UP, dot(k_t, toks[UP]))
    toks[GATE] = (key_back * key_up * slopes).astype(BF)
    begin(0, GATE, dot(k_t, toks[GATE]))
    pump(0, DOWN)
    curves = sig * (1.0 - sig) * (2.0 + key_gate * (1.0 - 2.0 * sig))
    saved[0] = act
    saved[1] = key_up * slopes
    pump(0, UP)
    pump(0, DOWN)
    saved[2] = key_back * slopes
    saved[3] = key_back * key_up * curves
    pump(0, GATE)
    pump(0, UP)
    pump(0, DOWN)
    w_t[DOWN] = wd_ref[...].T
    pump(0, GATE)
    pump(0, UP)
    pump(0, DOWN)
    w_t[UP] = wu_ref[...].T
    pump(0, GATE)
    pump(0, UP)
    pump(0, DOWN)
    w_t[GATE] = wg_ref[...].T

    inverse = {}

    def ortho_start(matrix):
        moment = total(0, matrix).astype(F32)
        inverse[matrix] = 1.0 / jnp.sqrt(total_of(moment * moment) + EPSILON)
        xs[matrix, 0] = (moment * inverse[matrix]).astype(BF)

    def ortho_step(matrix, number):
        current = xs[matrix, number]
        gram = dot_bt(current, current).astype(BF)
        poly = (NS_SECOND * gram.astype(F32) + NS_THIRD * dot(gram, gram)).astype(BF)
        grams[matrix, number] = gram
        polys[matrix, number] = poly
        following = (NS_FIRST * current.astype(F32) + dot(poly, current)).astype(BF)
        if number + 1 < NS_STEPS:
            xs[matrix, number + 1] = following
        else:
            new_t[matrix] = (w_t[matrix] + following.astype(F32)).astype(BF)

    def ortho(matrix):
        ortho_start(matrix)
        for number in range(NS_STEPS):
            ortho_step(matrix, number)

    def tick(number, *matrices):
        for matrix in matrices:
            pump(number, matrix)

    tick(0, GATE, UP, DOWN)
    q = q_ref[...]
    q_t = q.T
    o_t = o_ref[...].T
    tick(0, GATE, UP, DOWN)
    ortho(DOWN)
    tick(0, GATE, UP)
    query_back = dot(o_ref[...], new_t[DOWN])
    ortho(UP)
    tick(0, GATE)
    query_up = dot(q, new_t[UP])
    ortho(GATE)

    query_gate = dot(q, new_t[GATE])
    sig = jax.nn.sigmoid(query_gate)
    act = query_gate * sig
    slopes = sig * (1.0 + query_gate * (1.0 - sig))
    begin(1, DOWN, dot(o_t, (act * query_up).astype(BF)))
    qgate_tok = (query_back * query_up * slopes).astype(BF)
    begin(1, GATE, dot(q_t, qgate_tok))
    tick(1, DOWN)
    qup_tok = (query_back * act).astype(BF)
    begin(1, UP, dot(q_t, qup_tok))
    tick(1, GATE, DOWN)
    queries = dot_bt(qup_tok, new_t[UP])
    tick(1, UP, GATE, DOWN)
    dq_ref[...] = (queries + dot_bt(qgate_tok, new_t[GATE])).astype(BF)
    tick(1, UP, GATE, DOWN)
    scaled = (rates * v_ref[...].astype(F32)).astype(BF)
    k = k_ref[...]
    for _ in range(3):
        tick(1, UP, GATE, DOWN)

    def unortho(matrix):
        upstream_half = total(1, matrix)
        upstream = upstream_half.astype(F32)
        for number in reversed(range(NS_STEPS)):
            current = xs[matrix, number]
            poly_cot = dot_bt(current, upstream_half)
            poly_cot = poly_cot + poly_cot.T
            mixed = dot(poly_cot.astype(BF), grams[matrix, number])
            sym = (NS_SECOND * poly_cot + NS_THIRD * (mixed + mixed.T)).astype(BF)
            upstream = NS_FIRST * upstream + dot(
                jnp.concatenate([polys[matrix, number], sym], axis=1),
                jnp.concatenate([upstream_half, current], axis=0),
            )
            upstream_half = upstream.astype(BF)
        moment = total(0, matrix).astype(F32)
        inv = inverse[matrix]
        return (upstream * inv - moment * (total_of(upstream * moment) * (inv * inv * inv))).astype(BF)

    mdown = unortho(DOWN)
    tick(1, UP, GATE)
    back_act = dot(scaled, mdown)
    values = dot_bt(toks[DOWN], mdown)
    mgate = unortho(GATE)
    tick(1, UP)
    back_gate = dot(k, mgate)
    keys = dot_bt(toks[GATE], mgate)
    back_keyup = (back_gate * saved[2] + back_act * saved[0]).astype(BF)
    keys = keys + dot(back_keyup, wu_ref[...].astype(BF))
    keygate_part = back_act * saved[1] + back_gate * saved[3]
    keyback_part = back_gate * saved[1]
    mup = unortho(UP)
    back_up = dot(k, mup)
    back_keyback = (keyback_part + back_up * saved[0]).astype(BF)
    values = values + dot(back_keyback, wd_ref[...].astype(BF))
    dv_ref[...] = (rates * values).astype(BF)
    rates_grad = jnp.sum(v_ref[...].astype(F32) * values, axis=1, keepdims=True)
    dr_ref[...] = jnp.broadcast_to(rates_grad, (rates_grad.shape[0], 128)).T[:1]
    back_keygate = (keygate_part + back_up * saved[2]).astype(BF)
    keys = keys + dot_bt(toks[UP], mup) + dot(back_keygate, wg_ref[...].astype(BF))
    dk_ref[...] = keys.astype(BF)
    for chunk in every:
        for copy in chunk.sent:
            copy.wait_send()


def handing(*refs):
    for source, target in zip(refs[:4], refs[4:]):
        target[...] = source[...]


def on_device(n_view, n_tok, q, k, v, r, o, wg, wu, wd):
    rows, features = q.shape
    hidden = wg.shape[0]
    tok_bits, view_bits = bits_of("tok", n_tok), bits_of("view", n_view)
    orders = (tok_bits + view_bits, tok_bits[:1] + view_bits[:1] + tok_bits[1:] + view_bits[1:])
    levels = len(orders[0])
    n_halved = min(HALVINGS, levels - 1)
    n_exchanged = levels - n_halved
    width = hidden // 2
    segment = features >> n_halved
    lead = (2, 3, 2)
    vmem = pl.BlockSpec(memory_space=pltpu.VMEM)
    steps = levels + n_halved
    outs = pl.pallas_call(
        functools.partial(kernel, orders, n_halved, n_exchanged),
        out_shape=(
            jax.ShapeDtypeStruct((rows, features), BF),
            jax.ShapeDtypeStruct((rows, features), BF),
            jax.ShapeDtypeStruct((rows, features), BF),
            jax.ShapeDtypeStruct((1, rows), F32),
        ),
        in_specs=[vmem] * 8,
        out_specs=(vmem,) * 4,
        scratch_shapes=[
            pltpu.VMEM(lead + (features, width), BF),
            pltpu.VMEM(lead + (features, width), BF),
            pltpu.VMEM((3, NS_STEPS, features, hidden), BF),
            pltpu.VMEM((3, NS_STEPS, features, features), BF),
            pltpu.VMEM((3, NS_STEPS, features, features), BF),
            pltpu.VMEM((3, features, hidden), BF),
            pltpu.VMEM((3, features, hidden), F32),
            pltpu.VMEM((4, rows, hidden), F32),
            pltpu.VMEM((3, rows, hidden), BF),
            pltpu.SemaphoreType.DMA(lead + (steps,)),
            pltpu.SemaphoreType.DMA(lead + (steps,)),
        ]
        + [pltpu.VMEM(lead + (features >> (level + 1), width), BF) for level in range(n_halved)]
        + [pltpu.VMEM(lead + (segment, width), BF) for _ in range(n_exchanged)]
        + [pltpu.VMEM(lead + (segment, width), BF) for _ in range(n_exchanged - 1)],
        compiler_params=pltpu.CompilerParams(
            collective_id=0, has_side_effects=True, vmem_limit_bytes=60 * 1024 * 1024
        ),
    )(q, k, v, r.reshape(1, rows), o, wg, wu, wd)
    outs = pl.pallas_call(
        handing,
        out_shape=tuple(jax.ShapeDtypeStruct(out.shape, out.dtype) for out in outs),
        in_specs=[vmem] * 4,
        out_specs=(vmem,) * 4,
    )(*outs)
    return (outs[0], outs[1], outs[2], outs[3].reshape(rows))


def solution(mesh):
    rows = P(("group", "view", "tok"), None)
    flat = P(("group", "view", "tok"))
    return jax.shard_map(
        functools.partial(on_device, mesh.shape["view"], mesh.shape["tok"]),
        mesh=mesh,
        in_specs=(rows, rows, rows, flat, rows, P(), P(), P()),
        out_specs=(rows, rows, rows, flat),
        check_vma=False,
    )
```
